32 devices in a mesh: fsdp: 4 (over y, x), ctx: 4 (over z), tp: 2 (over core).
Axes of the slice: x: 2, y: 2, z: 4, core: 2. Of those that a mesh axis runs over, the one named last changes fastest.
Arguments:
- tokens: bfloat16 [12288, 896], P(('fsdp', 'ctx')), may hold values from -6 to 6
- cotangent: bfloat16 [12288, 896], P(('fsdp', 'ctx')), may hold values from -6 to 6
- seq_lengths: int32 [4, 3], P('fsdp'), may hold values from 1024 to 1024, as said below
- attn_gain: bfloat16 [896], P('fsdp'), may hold values from 0.5 to 1.5
- qkv_weight: bfloat16 [896, 1152], P('fsdp', 'tp'), may hold values from -0.1875 to 0.1875
- joined_bias: bfloat16 [2, 576], P('tp', 'fsdp'), may hold values from -0.3125 to 0.3125
- out_weight: bfloat16 [896, 896], P('tp', 'fsdp'), may hold values from -6 to 6
- mlp_gain: bfloat16 [896], P('fsdp'), may hold values from 0.5 to 1.5
- gate_up_weight: bfloat16 [896, 2, 4864], P('fsdp', None, 'tp'), may hold values from -0.1875 to 0.1875
- down_weight: bfloat16 [4864, 896], P('tp', 'fsdp'), may hold values from -0.078125 to 0.078125
Outputs:
- layer_out: bfloat16 [12288, 896], P(('fsdp', 'ctx'))
- token_grad: bfloat16 [12288, 896], P(('fsdp', 'ctx'))
- attn_gain_grad: float32 [896], P('fsdp')
- qkv_weight_grad: float32 [896, 1152], P('fsdp', 'tp')
- qkv_bias_grad: float32 [2, 576], P('tp', 'fsdp')
- out_weight_grad: float32 [896, 896], P('tp', 'fsdp')
- mlp_gain_grad: float32 [896], P('fsdp')
- gate_up_grad: float32 [896, 2, 4864], P('fsdp', None, 'tp')
- down_grad: float32 [4864, 896], P('tp', 'fsdp')
The draws below stay inside these ranges and needn't reach their ends.
Inputs may be any that keep to these rules, and one draw needn't show every extreme that they name: `seq_lengths`: each row holds 3 lengths, each a multiple of 4, summing to 3072; in some row all lengths but the last are 1024.
All inputs are finite; a program needn't handle non-finite values.
Results may differ from the reference program's by a relative error of at most 0.024.
Values may be sent and summed in bfloat16 or wider, within the bound.
A program may use at most 128 MiB of HBM per device.

```python
import math
import jax
import jax.numpy as jnp
from jax import lax

D = 896
FF = 4864
QUERY_HEADS = 14
KEY_VALUE_HEADS = 2
HEAD_SIZE = 64
TOK_DEV = 768
SEQS = 3
MIN_SEQ = 1024
TOKENS = 12288
JOINED_COLUMNS = 1152
N_FSDP = 4
N_CTX = 4


def draw_seq_lengths(key, part):
    key = jax.random.fold_in(key, 17)
    cut_key, pick_key = jax.random.split(key)
    least_piece = MIN_SEQ // N_CTX
    spare_rows = TOK_DEV - SEQS * least_piece
    cut_points = jnp.sort(jax.random.randint(cut_key, (N_FSDP, SEQS - 1), 0, spare_rows + 1), axis=1)
    chosen = jax.random.randint(pick_key, (), 0, N_FSDP)
    cut_points = jnp.where(jnp.arange(N_FSDP)[:, None] == chosen, 0, cut_points).astype(jnp.int32)
    boundaries = jnp.concatenate([jnp.zeros((N_FSDP, 1), jnp.int32), cut_points, jnp.full((N_FSDP, 1), spare_rows, jnp.int32)], axis=1)
    return ((boundaries[:, 1:] - boundaries[:, :-1] + least_piece) * N_CTX).astype(jnp.int32)


def levels(rng, shape, cuts, low, top_value):
    loudness, own = 1.0, jax.random.fold_in(rng, 6)
    for dim, parts in cuts:
        steps = jnp.exp(jax.random.uniform(jax.random.fold_in(own, dim), (parts,), jnp.float32, low / len(cuts), top_value / len(cuts)))
        loudness = loudness * jnp.repeat(steps, shape[dim] // parts).reshape([-1 if axis == dim else 1 for axis in range(len(shape))])
    return loudness


def gaussian(own_key, shape, spread, reach, shards=(), kind=jnp.bfloat16):
    level = levels(own_key, shape, shards, -0.22, 0.18) if shards else 1.0
    array = jax.random.normal(own_key, shape, jnp.float32) * spread * level
    return jnp.minimum(jnp.maximum(array, -reach), reach).astype(kind)


def setup_inputs(seed: int = 0) -> dict:
    arg_keys = jax.random.split(jax.random.key(seed), 11)
    return {
        "tokens": gaussian(arg_keys[0], (TOKENS, D), 1.0, 6.0, ((0, 16),)),
        "cotangent": gaussian(arg_keys[1], (TOKENS, D), 1.0, 6.0, ((0, 16),)),
        "seq_lengths": draw_seq_lengths(jax.random.fold_in(arg_keys[10], 71), 0),
        "attn_gain": jnp.clip(1.0 + 0.1 * jax.random.normal(arg_keys[3], (D,), jnp.float32), 0.5, 1.5).astype(jnp.bfloat16),
        "qkv_weight": gaussian(arg_keys[4], (D, JOINED_COLUMNS), D ** -0.5, 0.1875, ((0, 4), (1, 2))),
        "joined_bias": gaussian(arg_keys[5], (KEY_VALUE_HEADS, JOINED_COLUMNS // KEY_VALUE_HEADS), 0.02, 0.3125, ((0, 2), (1, 4))),
        "out_weight": gaussian(arg_keys[6], (QUERY_HEADS * HEAD_SIZE, D), (max(1, QUERY_HEADS * HEAD_SIZE // MIN_SEQ)) ** -0.5, 6.0, ((0, 2), (1, 4))),
        "mlp_gain": jnp.clip(1.0 + 0.1 * jax.random.normal(arg_keys[7], (D,), jnp.float32), 0.5, 1.5).astype(jnp.bfloat16),
        "gate_up_weight": gaussian(arg_keys[8], (D, 2, FF), D ** -0.5, 0.1875, ((0, 4), (2, 2))),
        "down_weight": gaussian(arg_keys[9], (FF, D), FF ** -0.5, 0.078125, ((0, 2), (1, 4))),
    }


EPSILON = 1e-06
SCORE_SCALE = 0.125
THETA = 1000000.0
MASKED = -1e+30
HIGHEST = lax.Precision.HIGHEST

@jax.custom_vjp
def low(v):
    return lax.optimization_barrier(v.astype(jnp.bfloat16)).astype(jnp.float32)

@jax.custom_vjp
def low_back(v):
    return v

def low_keep(v):
    return (low(v), None)

def low_pass(kept, grad):
    return (grad,)

def back_keep(v):
    return (v, None)

def back_low(kept, grad):
    return (low(grad),)
low.defvjp(low_keep, low_pass)
low_back.defvjp(back_keep, back_low)

def places(row_ids, block_ids, pieces):
    seq_count = pieces.shape[0]
    seq_ends = jnp.cumsum(pieces, dtype=jnp.int32)
    starts = seq_ends - pieces
    sequence_index = lax.optimization_barrier(jnp.sum((row_ids[:, None] >= seq_ends[None, :seq_count - 1]).astype(jnp.int32), axis=1, dtype=jnp.int32))
    chosen = sequence_index[:, None] == jnp.arange(seq_count, dtype=jnp.int32)[None, :]
    own_piece = lax.optimization_barrier(jnp.sum(jnp.where(chosen, pieces[None, :], 0), axis=1, dtype=jnp.int32))
    first_row = lax.optimization_barrier(jnp.sum(jnp.where(chosen, starts[None, :], 0), axis=1, dtype=jnp.int32))
    return (sequence_index, block_ids * own_piece + row_ids - first_row)

def turning(token_position, head_width):
    half_width = head_width // 2
    frequency = jnp.exp(jnp.arange(half_width, dtype=jnp.float32) * (-2.0 * math.log(THETA) / head_width))
    angles = token_position.astype(jnp.float32)[:, None] * frequency[None, :]
    cosine_half = jnp.cos(angles)
    sine_half = jnp.sin(angles)
    return (jnp.concatenate([cosine_half, cosine_half], axis=-1), jnp.concatenate([sine_half, sine_half], axis=-1))

def rotate(vectors, cosine_table, sine_table):
    half_width = vectors.shape[-1] // 2
    turned = jnp.concatenate([-vectors[..., half_width:], vectors[..., :half_width]], axis=-1)
    return vectors * cosine_table + turned * sine_table

def rms_unit(vectors):
    return vectors * lax.rsqrt(lax.optimization_barrier(jnp.mean(vectors * vectors, axis=-1, keepdims=True)) + EPSILON)

def attend(query_block, seq_block, pos_block, key_rows, value_rows, key_seq, key_pos):
    scores = jnp.einsum('qtjd,ktd->tjqk', query_block, key_rows, precision=HIGHEST) * SCORE_SCALE
    scores = low_back(scores)
    allowed = (seq_block[:, None] == key_seq[None, :]) & (key_pos[None, :] <= pos_block[:, None])
    scores = jnp.where(allowed, scores, MASKED)
    soft_weights = low(jax.nn.softmax(scores, axis=-1))
    return jnp.einsum('tjqk,ktd->qtjd', soft_weights, value_rows, precision=HIGHEST)

def layer(params, inputs, sequence_index, token_position):
    gain_one, qkv_full, bias_full, out_full, gain_two, gate_up_full, down_full = params
    count_of_rows = inputs.shape[0]
    heads_per_group = QUERY_HEADS // KEY_VALUE_HEADS
    normed_one = low(rms_unit(inputs) * gain_one)
    projected_rows = low_back(jnp.dot(normed_one, qkv_full, precision=HIGHEST) + bias_full.reshape(-1))
    projected_rows = projected_rows.reshape(count_of_rows, KEY_VALUE_HEADS, heads_per_group + 2, HEAD_SIZE)
    cosine_table, sine_table = turning(token_position, HEAD_SIZE)
    query_rows = low(rotate(projected_rows[:, :, :heads_per_group], cosine_table[:, None, None], sine_table[:, None, None]))
    key_rows = low(rotate(projected_rows[:, :, heads_per_group], cosine_table[:, None], sine_table[:, None]))
    value_rows = low(projected_rows[:, :, heads_per_group + 1])
    rows_per_block = min(512, count_of_rows)

    def single_block(block_item):
        return attend(block_item[0], block_item[1], block_item[2], key_rows, value_rows, sequence_index, token_position)
    mixed_output = lax.map(jax.checkpoint(single_block), (query_rows.reshape(count_of_rows // rows_per_block, rows_per_block, KEY_VALUE_HEADS, heads_per_group, HEAD_SIZE), sequence_index.reshape(-1, rows_per_block), token_position.reshape(-1, rows_per_block)))
    mixed_output = low(low_back(mixed_output.reshape(count_of_rows, QUERY_HEADS * HEAD_SIZE)))
    hidden = inputs + low_back(jnp.dot(mixed_output, out_full, precision=HIGHEST))
    normed_two = low(rms_unit(hidden) * gain_two)
    gate_up = low_back(jnp.einsum('td,dcf->tcf', normed_two, gate_up_full, precision=HIGHEST))
    activated = low(jax.nn.silu(gate_up[:, 0]) * gate_up[:, 1])
    return hidden + low_back(jnp.dot(activated, down_full, precision=HIGHEST))

def reference(tokens, cotangent, seq_lengths, attn_gain, qkv_weight, joined_bias, out_weight, mlp_gain, gate_up_weight, down_weight):
    params = (attn_gain.astype(jnp.float32), qkv_weight.astype(jnp.float32), joined_bias.astype(jnp.float32), out_weight.astype(jnp.float32), mlp_gain.astype(jnp.float32), gate_up_weight.astype(jnp.float32), down_weight.astype(jnp.float32))
    group_rows = TOK_DEV * N_CTX
    row_ids = jnp.arange(group_rows, dtype=jnp.int32)

    def per_group(totals, group_item):
        inputs, grad_out, lengths = group_item
        sequence_index, token_position = places(row_ids % TOK_DEV, row_ids // TOK_DEV, (lengths // N_CTX).astype(jnp.int32))

        def forward(weights, activations):
            return layer(weights, activations, sequence_index, token_position)
        result, pullback = jax.vjp(forward, params, inputs)
        weight_grads, input_grad = pullback(grad_out)
        totals = jax.tree.map(jnp.add, totals, weight_grads)
        return (totals, (result.astype(jnp.bfloat16), input_grad.astype(jnp.bfloat16)))
    zero_grads = jax.tree.map(jnp.zeros_like, params)
    stacked = (tokens.astype(jnp.float32).reshape(N_FSDP, group_rows, D), cotangent.astype(jnp.float32).reshape(N_FSDP, group_rows, D), seq_lengths)
    totals, (results, input_grads) = lax.scan(per_group, zero_grads, stacked)
    return (results.reshape(N_FSDP * group_rows, D), input_grads.reshape(N_FSDP * group_rows, D), totals[0], totals[1], totals[2], totals[3], totals[4], totals[5], totals[6])
```

```python
import math

import jax
import jax.numpy as jnp
from jax import lax
from jax.experimental import pallas as pl
from jax.experimental.pallas import tpu as pltpu
from jax.sharding import PartitionSpec as P

HEAD_SIZE = 64


EPSILON = 1e-06
SCORE_SCALE = 0.125
THETA = 1000000.0
MASKED = -1e30


def places(row_ids, block_ids, pieces):
    seq_count = pieces.shape[0]
    seq_ends = jnp.cumsum(pieces, dtype=jnp.int32)
    starts = seq_ends - pieces
    sequence_index = jnp.sum(
        (row_ids[:, None] >= seq_ends[None, : seq_count - 1]).astype(jnp.int32),
        axis=1,
        dtype=jnp.int32,
    )
    chosen = sequence_index[:, None] == jnp.arange(seq_count, dtype=jnp.int32)[None, :]
    own_piece = jnp.sum(jnp.where(chosen, pieces[None, :], 0), axis=1, dtype=jnp.int32)
    first_row = jnp.sum(jnp.where(chosen, starts[None, :], 0), axis=1, dtype=jnp.int32)
    return (sequence_index, block_ids * own_piece + row_ids - first_row)


def turning(token_position, head_width):
    half_width = head_width // 2
    frequency = jnp.exp(
        jnp.arange(half_width, dtype=jnp.float32) * (-2.0 * math.log(THETA) / head_width)
    )
    angles = token_position.astype(jnp.float32)[:, None] * frequency[None, :]
    cosine_half = jnp.cos(angles)
    sine_half = jnp.sin(angles)
    return (
        jnp.concatenate([cosine_half, cosine_half], axis=-1),
        jnp.concatenate([sine_half, sine_half], axis=-1),
    )


def rotate(vectors, cosine_table, sine_table):
    half_width = vectors.shape[-1] // 2
    turned = jnp.concatenate([-vectors[..., half_width:], vectors[..., :half_width]], axis=-1)
    return vectors * cosine_table + turned * sine_table


def unrotate(gradient, cosine_table, sine_table):
    half_width = gradient.shape[-1] // 2
    weighted = gradient * sine_table
    turned = jnp.concatenate([weighted[..., half_width:], -weighted[..., :half_width]], axis=-1)
    return gradient * cosine_table + turned


def norm_forward(vectors, gain_row):
    inverse = lax.rsqrt(jnp.mean(vectors * vectors, axis=-1, keepdims=True) + EPSILON)
    unit_rows = vectors * inverse
    return (unit_rows, inverse, unit_rows * gain_row)


def norm_backward(upstream, unit_rows, inverse, gain_row):
    scaled = upstream * gain_row
    back = inverse * (scaled - unit_rows * jnp.mean(scaled * unit_rows, axis=-1, keepdims=True))
    return (back, jnp.sum(upstream * unit_rows, axis=0))


MIN_SEQ = 1024
VMEM_LIMIT = 48 * 1024 * 1024


def nt_dot(left, right):
    return lax.dot_general(left, right, (((1,), (1,)), ((), ())), preferred_element_type=jnp.float32)


def nn_dot(left, right):
    return lax.dot_general(left, right, (((1,), (0,)), ((), ())), preferred_element_type=jnp.float32)


def load_pairs(pair_ref):
    chunks = pair_ref.shape[0]
    key_t = jnp.concatenate([pair_ref[j, :HEAD_SIZE, :] for j in range(chunks)], axis=1)
    value_t = jnp.concatenate([pair_ref[j, HEAD_SIZE:, :] for j in range(chunks)], axis=1)
    return key_t, value_t


def flip(block):
    return block.astype(jnp.float32).T.astype(jnp.bfloat16)


def causal_bias(me, keys, width):
    key_pos = lax.broadcasted_iota(jnp.int32, (keys, width), 0)
    query_pos = lax.broadcasted_iota(jnp.int32, (keys, width), 1) + me * width
    return jnp.where(key_pos <= query_pos, 0.0, MASKED)


def attend_kernel(me_ref, query_ref, pair_ref, out_ref, log_ref):
    width = query_ref.shape[1]
    heads = query_ref.shape[0] // HEAD_SIZE
    key_t, value_t = load_pairs(pair_ref)
    key = flip(key_t)
    bias = causal_bias(me_ref[0], key.shape[0], width)
    for h in range(heads):
        rows = slice(h * HEAD_SIZE, (h + 1) * HEAD_SIZE)
        scores = nn_dot(key, query_ref[rows, :]) + bias
        peak = jnp.max(scores, axis=0, keepdims=True)
        soft = jnp.exp(scores - peak)
        total = jnp.sum(soft, axis=0, keepdims=True)
        soft = (soft * (1.0 / total)).astype(jnp.bfloat16)
        out_ref[rows, :] = nn_dot(value_t, soft).astype(jnp.bfloat16)
        log_ref[h : h + 1, :] = peak + jnp.log(total)
    log_ref[heads:, :] = jnp.zeros_like(log_ref[heads:, :])


def attend_back_kernel(me_ref, query_ref, pair_ref, log_ref, grad_ref, query_grad_ref, pair_grad_ref):
    width = query_ref.shape[1]
    heads = query_ref.shape[0] // HEAD_SIZE
    key_t, value_t = load_pairs(pair_ref)
    key, value = flip(key_t), flip(value_t)
    bias = causal_bias(me_ref[0], key.shape[0], width)
    key_grad = jnp.zeros(key.shape, jnp.float32)
    value_grad = jnp.zeros(key.shape, jnp.float32)
    for h in range(heads):
        rows = slice(h * HEAD_SIZE, (h + 1) * HEAD_SIZE)
        query_t, grad_t = query_ref[rows, :], grad_ref[rows, :]
        soft = jnp.exp(nn_dot(key, query_t) + bias - log_ref[h : h + 1, :])
        prob_grad = nn_dot(value, grad_t)
        delta = jnp.sum(soft * prob_grad, axis=0, keepdims=True)
        score_grad = (soft * (prob_grad - delta)).astype(jnp.bfloat16)
        query_grad_ref[rows, :] = nn_dot(key_t, score_grad)
        key_grad = key_grad + nt_dot(score_grad, query_t)
        value_grad = value_grad + nt_dot(soft.astype(jnp.bfloat16), grad_t)
    both = jnp.concatenate([key_grad, value_grad], axis=1).astype(jnp.bfloat16)
    for j in range(pair_grad_ref.shape[0]):
        pair_grad_ref[j] = both[j * width : (j + 1) * width]


def even_attention(query_t, pairs_t, width):
    depth, rows = query_t.shape
    ctx = pairs_t.shape[0]
    me = lax.axis_index("ctx").astype(jnp.int32).reshape(1)
    scalar = pl.BlockSpec(memory_space=pltpu.SMEM)
    wide = pl.BlockSpec((depth, width), lambda s: (0, s))
    pair = pl.BlockSpec((ctx, 2 * HEAD_SIZE, width), lambda s: (0, 0, s))
    logs = pl.BlockSpec((8, width), lambda s: (0, s))
    params = pltpu.CompilerParams(vmem_limit_bytes=VMEM_LIMIT)
    mixed_t, log_total = pl.pallas_call(
        attend_kernel,
        grid=(rows // width,),
        in_specs=[scalar, wide, pair],
        out_specs=[wide, logs],
        out_shape=[
            jax.ShapeDtypeStruct((depth, rows), jnp.bfloat16),
            jax.ShapeDtypeStruct((8, rows), jnp.float32),
        ],
        compiler_params=params,
        name="attend",
    )(me, query_t, pairs_t)

    def back(mixed_back_t):
        return pl.pallas_call(
            attend_back_kernel,
            grid=(rows // width,),
            in_specs=[scalar, wide, pair, logs, wide],
            out_specs=[wide, pl.BlockSpec((ctx, width, 2 * HEAD_SIZE), lambda s: (0, s, 0))],
            out_shape=[
                jax.ShapeDtypeStruct((depth, rows), jnp.float32),
                jax.ShapeDtypeStruct((ctx, rows, 2 * HEAD_SIZE), jnp.bfloat16),
            ],
            compiler_params=params,
            name="attend_back",
        )(me, query_t, pairs_t, log_total, mixed_back_t)

    return mixed_t, back


def ragged_attention(query_t, pairs_t, query_seq, query_pos, pieces):
    ctx = pairs_t.shape[0]
    depth, count_of_rows = query_t.shape
    heads = depth // HEAD_SIZE
    query_rows = query_t.reshape(heads, HEAD_SIZE, count_of_rows).transpose(2, 0, 1)
    pairs = pairs_t.transpose(0, 2, 1).reshape(ctx * count_of_rows, 2 * HEAD_SIZE)
    group_rows = pairs.shape[0]
    key_ids = jnp.arange(group_rows, dtype=jnp.int32)
    key_seq, key_pos = places(key_ids % count_of_rows, key_ids // count_of_rows, pieces)
    key_width = min(512, group_rows)
    block_count = group_rows // key_width

    def scores_at(block_no):
        row_start = block_no * key_width
        pair_rows = lax.dynamic_slice_in_dim(pairs, row_start, key_width, 0)
        seq_part = lax.dynamic_slice_in_dim(key_seq, row_start, key_width, 0)
        pos_part = lax.dynamic_slice_in_dim(key_pos, row_start, key_width, 0)
        allowed = (query_seq[:, None] == seq_part[None, :]) & (
            pos_part[None, :] <= query_pos[:, None]
        )
        key_part = pair_rows[:, :HEAD_SIZE]
        scores = jnp.einsum(
            "qhd,kd->hqk", query_rows, key_part, preferred_element_type=jnp.float32
        )
        return (scores, allowed[None], key_part, pair_rows[:, HEAD_SIZE:])

    def peak_step(block_no, running):
        run_peak, run_total = running
        scores, allowed, key_part, value_part = scores_at(block_no)
        scores = jnp.where(allowed, scores, MASKED)
        new_peak = jnp.maximum(run_peak, jnp.max(scores, axis=-1))
        run_total = run_total * jnp.exp(run_peak - new_peak) + jnp.sum(
            jnp.where(allowed, jnp.exp(scores - new_peak[..., None]), 0.0), axis=-1
        )
        return (new_peak, run_total)

    start_peak = jnp.full((heads, count_of_rows), MASKED, jnp.float32)
    run_peak, run_total = lax.fori_loop(
        0, block_count, peak_step, (start_peak, jnp.zeros_like(start_peak))
    )
    log_total = run_peak + jnp.log(run_total)

    def soft_at(scores, allowed):
        return jnp.where(allowed, jnp.exp(scores - log_total[..., None]), 0.0)

    def output_step(block_no, running):
        scores, allowed, key_part, value_part = scores_at(block_no)
        soft_low = soft_at(scores, allowed).astype(jnp.bfloat16)
        return running + jnp.einsum(
            "hqk,kd->qhd", soft_low, value_part, preferred_element_type=jnp.float32
        )

    attended = lax.fori_loop(
        0, block_count, output_step, jnp.zeros((count_of_rows, heads, HEAD_SIZE), jnp.float32)
    )
    mixed_t = attended.transpose(1, 2, 0).reshape(depth, count_of_rows).astype(jnp.bfloat16)

    def back(mixed_back_t):
        mixed_back = mixed_back_t.reshape(heads, HEAD_SIZE, count_of_rows).transpose(2, 0, 1)
        correction = jnp.einsum("qhd,qhd->hq", mixed_back.astype(jnp.float32), attended)

        def grad_step(block_no, running):
            query_grad, pair_grads = running
            scores, allowed, key_part, value_part = scores_at(block_no)
            soft_part = soft_at(scores, allowed)
            prob_grad = jnp.einsum(
                "qhd,kd->hqk", mixed_back, value_part, preferred_element_type=jnp.float32
            )
            score_grad = (soft_part * (prob_grad - correction[..., None])).astype(jnp.bfloat16)
            query_grad = query_grad + jnp.einsum(
                "hqk,kd->qhd", score_grad, key_part, preferred_element_type=jnp.float32
            )
            key_grad = jnp.einsum(
                "hqk,qhd->kd", score_grad, query_rows, preferred_element_type=jnp.float32
            )
            value_grad = jnp.einsum(
                "hqk,qhd->kd",
                soft_part.astype(jnp.bfloat16),
                mixed_back,
                preferred_element_type=jnp.float32,
            )
            pair_grads = lax.dynamic_update_slice_in_dim(
                pair_grads,
                jnp.concatenate([key_grad, value_grad], axis=-1),
                block_no * key_width,
                0,
            )
            return (query_grad, pair_grads)

        start_grads = (
            jnp.zeros((count_of_rows, heads, HEAD_SIZE), jnp.float32),
            jnp.zeros((group_rows, 2 * HEAD_SIZE), jnp.float32),
        )
        query_grad, pair_grads = lax.fori_loop(0, block_count, grad_step, start_grads)
        query_grad_t = query_grad.transpose(1, 2, 0).reshape(depth, count_of_rows)
        return query_grad_t, pair_grads.astype(jnp.bfloat16).reshape(
            ctx, count_of_rows, 2 * HEAD_SIZE
        )

    return mixed_t, back


def dot32(spec, left, right):
    return jnp.einsum(spec, left, right, preferred_element_type=jnp.float32)


def pair_sum(partial):
    low = partial.astype(jnp.bfloat16)
    if lax.axis_size("tp") != 2:
        return lax.psum(low, "tp").astype(jnp.float32)
    other = lax.ppermute(low, "tp", [(0, 1), (1, 0)])
    return low.astype(jnp.float32) + other.astype(jnp.float32)


def pair_join(half):
    if lax.axis_size("tp") != 2:
        return lax.all_gather(half, "tp", axis=0, tiled=True)
    other = lax.ppermute(half, "tp", [(0, 1), (1, 0)])
    first = lax.axis_index("tp") == 0
    return jnp.concatenate([jnp.where(first, half, other), jnp.where(first, other, half)], axis=0)


def pair_half(rows):
    count = rows.shape[0] // lax.axis_size("tp")
    return lax.dynamic_slice_in_dim(rows, lax.axis_index("tp") * count, count, 0)


PLANE = ("fsdp", "tp")


def body(
    tokens,
    cotangent,
    seq_lengths,
    attn_gain,
    qkv_weight,
    joined_bias,
    out_weight,
    mlp_gain,
    gate_up_weight,
    down_weight,
):
    fsdp_size = lax.axis_size("fsdp")
    ctx_size = lax.axis_size("ctx")
    rows = tokens.shape[0]
    part, columns = qkv_weight.shape
    model = part * fsdp_size
    slots = columns // HEAD_SIZE
    heads = slots - 2
    depth = heads * HEAD_SIZE
    bias_part = joined_bias.shape[1]
    hidden_units = down_weight.shape[0]
    ff = hidden_units // fsdp_size

    small = jnp.concatenate(
        [
            jnp.pad(attn_gain[None], ((0, 0), (0, columns - part))),
            jnp.pad(mlp_gain[None], ((0, 0), (0, columns - part))),
            jnp.pad(joined_bias, ((0, 0), (0, columns - bias_part))),
            jnp.zeros((13, columns), jnp.bfloat16),
        ],
        axis=0,
    )
    packed = lax.all_gather(
        jnp.concatenate([qkv_weight, small], axis=0), "fsdp", axis=0, tiled=False
    )
    wide_qkv = packed[:, :part].reshape(model, columns)
    gain_one = packed[:, part, :part].reshape(model).astype(jnp.float32)
    gain_two = packed[:, part + 1, :part].reshape(model).astype(jnp.float32)
    bias_row = packed[:, part + 2, :bias_part].reshape(columns).astype(jnp.float32)

    pieces = seq_lengths[0] // ctx_size
    local_rows = jnp.arange(rows, dtype=jnp.int32)
    query_seq, query_pos = places(local_rows, lax.axis_index("ctx"), pieces)
    half = HEAD_SIZE // 2
    frequency = jnp.exp(
        jnp.arange(half, dtype=jnp.float32) * (-2.0 * math.log(THETA) / HEAD_SIZE)
    )
    angles = frequency[:, None] * query_pos.astype(jnp.float32)[None, :]
    cosine, sine = jnp.cos(angles)[None], jnp.sin(angles)[None]

    inputs = tokens.astype(jnp.float32)
    unit_one, inv_one, scaled_one = norm_forward(inputs, gain_one)
    normed_one = scaled_one.astype(jnp.bfloat16)
    projected = dot32("dc,td->ct", wide_qkv, normed_one) + bias_row[:, None]
    projected = projected.reshape(slots, HEAD_SIZE, rows)
    first, second = projected[: heads + 1, :half], projected[: heads + 1, half:]
    turned = jnp.concatenate(
        [first * cosine - second * sine, second * cosine + first * sine], axis=1
    ).astype(jnp.bfloat16)
    query_t = (turned[:heads] * SCORE_SCALE).reshape(depth, rows)
    pair_t = jnp.concatenate([turned[heads], projected[heads + 1].astype(jnp.bfloat16)], axis=0)
    pairs_t = lax.all_gather(pair_t, "ctx", axis=0, tiled=False)

    wide_out = lax.all_gather(out_weight, "fsdp", axis=1, tiled=True)
    gate_up_parts = gate_up_weight.reshape(part, 2, fsdp_size, ff).transpose(2, 0, 1, 3)
    gate_up_parts = lax.all_to_all(
        gate_up_parts.reshape(fsdp_size, part, 2 * ff), "fsdp", 0, 0, tiled=True
    )
    wide_gate_up = gate_up_parts.reshape(model, 2 * ff)
    down_parts = lax.all_to_all(
        down_weight.reshape(fsdp_size, ff, part), "fsdp", 0, 0, tiled=True
    )
    wide_down = down_parts.transpose(1, 0, 2).reshape(ff, model)
    cot_all = lax.all_gather(pair_half(cotangent), PLANE, axis=0, tiled=True)

    seqs = seq_lengths.shape[1]
    if rows * ctx_size == seqs * MIN_SEQ and (rows // seqs) % 128 == 0:
        mixed_t, attention_back = even_attention(query_t, pairs_t, rows // seqs)
    else:
        mixed_t, attention_back = ragged_attention(query_t, pairs_t, query_seq, query_pos, pieces)

    hidden = inputs + pair_sum(dot32("et,ed->td", mixed_t, wide_out))
    unit_two, inv_two, scaled_two = norm_forward(hidden, gain_two)
    normed_two = lax.all_gather(
        pair_half(scaled_two.astype(jnp.bfloat16)), PLANE, axis=0, tiled=True
    )
    gate_up = dot32("td,df->tf", normed_two, wide_gate_up)
    gate_in, up_in = gate_up[:, :ff], gate_up[:, ff:]
    sigmoid_gate = jax.nn.sigmoid(gate_in)
    activated = (gate_in * sigmoid_gate * up_in).astype(jnp.bfloat16)
    act_grad = dot32("td,fd->tf", cot_all, wide_down)
    gate_grad = act_grad * up_in * sigmoid_gate * (1.0 + gate_in * (1.0 - sigmoid_gate))
    up_grad = act_grad * gate_in * sigmoid_gate
    gate_up_back = jnp.concatenate([gate_grad, up_grad], axis=1).astype(jnp.bfloat16)
    normed_two_grad = lax.psum_scatter(
        dot32("tf,df->td", gate_up_back, wide_gate_up).astype(jnp.bfloat16),
        PLANE,
        scatter_dimension=0,
        tiled=True,
    )
    mlp_out = lax.psum_scatter(
        dot32("tf,fd->td", activated, wide_down).astype(jnp.bfloat16),
        PLANE,
        scatter_dimension=0,
        tiled=True,
    )
    layer_out = (hidden + pair_join(mlp_out).astype(jnp.float32)).astype(jnp.bfloat16)

    gate_up_grad = dot32("td,tf->df", normed_two, gate_up_back).astype(jnp.bfloat16)
    down_grad = dot32("tf,td->fd", activated, cot_all).astype(jnp.bfloat16)
    gate_up_grad = lax.psum_scatter(
        gate_up_grad.reshape(fsdp_size, part, 2 * ff), "ctx", scatter_dimension=1, tiled=True
    )
    gate_up_grad = lax.all_to_all(gate_up_grad, "fsdp", 0, 0, tiled=True)
    gate_up_grad = lax.all_gather(gate_up_grad, "ctx", axis=1, tiled=True)
    gate_up_total = (
        gate_up_grad.reshape(fsdp_size, part, 2, ff)
        .transpose(1, 2, 0, 3)
        .reshape(part, 2, hidden_units)
        .astype(jnp.float32)
    )
    down_grad = lax.psum_scatter(
        down_grad.reshape(ff, fsdp_size, part).transpose(1, 0, 2),
        "ctx",
        scatter_dimension=1,
        tiled=True,
    )
    down_grad = lax.all_to_all(down_grad, "fsdp", 0, 0, tiled=True)
    down_grad = lax.all_gather(down_grad, "ctx", axis=1, tiled=True)
    down_total = down_grad.reshape(hidden_units, part).astype(jnp.float32)

    hidden_norm_grad, mlp_gain_grad = norm_backward(
        pair_join(normed_two_grad).astype(jnp.float32), unit_two, inv_two, gain_two
    )
    hidden_grad = cotangent.astype(jnp.float32) + hidden_norm_grad
    attn_back = hidden_grad.astype(jnp.bfloat16)
    mixed_back_t = dot32("ed,td->et", wide_out, attn_back).astype(jnp.bfloat16)
    out_weight_grad = dot32("td,et->de", attn_back, mixed_t).astype(jnp.bfloat16)

    query_grad_t, pair_grads = attention_back(mixed_back_t)
    pair_own = lax.psum_scatter(pair_grads, "ctx", scatter_dimension=0, tiled=True)
    pair_own = pair_own.reshape(rows, 2 * HEAD_SIZE).astype(jnp.float32).T
    turned_grad = jnp.concatenate(
        [query_grad_t.reshape(heads, HEAD_SIZE, rows) * SCORE_SCALE, pair_own[None, :HEAD_SIZE]],
        axis=0,
    )
    first, second = turned_grad[:, :half], turned_grad[:, half:]
    turned_grad = jnp.concatenate(
        [first * cosine + second * sine, second * cosine - first * sine], axis=1
    )
    projected_back = (
        jnp.concatenate([turned_grad, pair_own[None, HEAD_SIZE:]], axis=0)
        .reshape(columns, rows)
        .astype(jnp.bfloat16)
    )
    normed_one_grad = pair_sum(dot32("ct,dc->td", projected_back, wide_qkv))
    input_norm_grad, attn_gain_grad = norm_backward(normed_one_grad, unit_one, inv_one, gain_one)
    token_grad = (hidden_grad + input_norm_grad).astype(jnp.bfloat16)

    qkv_bias_grad = jnp.sum(projected_back, axis=1, dtype=jnp.float32).astype(jnp.bfloat16)
    qkv_weight_grad = dot32("td,ct->dc", normed_one, projected_back).astype(jnp.bfloat16)
    wide_grads = jnp.concatenate([qkv_weight_grad, out_weight_grad], axis=1)
    wide_grads = wide_grads.reshape(fsdp_size, part, columns + depth)
    bias_back = qkv_bias_grad.reshape(fsdp_size, 1, bias_part)
    bias_back = jnp.pad(bias_back, ((0, 0), (0, 0), (0, columns + depth - bias_part)))
    bias_back = jnp.pad(bias_back, ((0, 0), (0, 15), (0, 0)))
    small_grads = jnp.concatenate([wide_grads, bias_back], axis=1)
    small_own = lax.psum_scatter(small_grads, "fsdp", scatter_dimension=0, tiled=True)[0]
    small_own = lax.psum(small_own, "ctx").astype(jnp.float32)
    gains = lax.psum(
        jnp.stack([attn_gain_grad, mlp_gain_grad], axis=0), ("fsdp", "ctx")
    )
    gains = lax.dynamic_slice_in_dim(gains, lax.axis_index("fsdp") * part, part, 1)
    return (
        layer_out,
        token_grad,
        gains[0],
        small_own[:part, :columns],
        small_own[part : part + 1, :bias_part],
        small_own[:part, columns:].T,
        gains[1],
        gate_up_total,
        down_total,
    )


def solution(mesh):
    placed = (
        P(("fsdp", "ctx"), None),
        P(("fsdp", "ctx"), None),
        P("fsdp", None),
        P("fsdp"),
        P("fsdp", "tp"),
        P("tp", "fsdp"),
        P("tp", "fsdp"),
        P("fsdp"),
        P("fsdp", None, "tp"),
        P("tp", "fsdp"),
    )
    return jax.shard_map(
        body,
        mesh=mesh,
        in_specs=placed,
        out_specs=(
            P(("fsdp", "ctx"), None),
            P(("fsdp", "ctx"), None),
            P("fsdp"),
            P("fsdp", "tp"),
            P("tp", "fsdp"),
            P("tp", "fsdp"),
            P("fsdp"),
            P("fsdp", None, "tp"),
            P("tp", "fsdp"),
        ),
        check_vma=False,
    )
```

```python
import math

import jax
import jax.numpy as jnp
from jax import lax
from jax.experimental import pallas as pl
from jax.experimental.pallas import tpu as pltpu
from jax.sharding import PartitionSpec as P

HEAD_SIZE = 64


EPSILON = 1e-06
SCORE_SCALE = 0.125
THETA = 1000000.0
MASKED = -1e30


def places(row_ids, block_ids, pieces):
    seq_count = pieces.shape[0]
    seq_ends = jnp.cumsum(pieces, dtype=jnp.int32)
    starts = seq_ends - pieces
    sequence_index = jnp.sum(
        (row_ids[:, None] >= seq_ends[None, : seq_count - 1]).astype(jnp.int32),
        axis=1,
        dtype=jnp.int32,
    )
    chosen = sequence_index[:, None] == jnp.arange(seq_count, dtype=jnp.int32)[None, :]
    own_piece = jnp.sum(jnp.where(chosen, pieces[None, :], 0), axis=1, dtype=jnp.int32)
    first_row = jnp.sum(jnp.where(chosen, starts[None, :], 0), axis=1, dtype=jnp.int32)
    return (sequence_index, block_ids * own_piece + row_ids - first_row)


def norm_forward(vectors, gain_row):
    inverse = lax.rsqrt(jnp.mean(vectors * vectors, axis=-1, keepdims=True) + EPSILON)
    unit_rows = vectors * inverse
    return (unit_rows, inverse, unit_rows * gain_row)


def norm_backward(upstream, unit_rows, inverse, gain_row):
    scaled = upstream * gain_row
    back = inverse * (scaled - unit_rows * jnp.mean(scaled * unit_rows, axis=-1, keepdims=True))
    return (back, jnp.sum(upstream * unit_rows, axis=0))


MIN_SEQ = 1024
VMEM_LIMIT = 48 * 1024 * 1024


def nt_dot(left, right):
    return lax.dot_general(left, right, (((1,), (1,)), ((), ())), preferred_element_type=jnp.float32)


def nn_dot(left, right):
    return lax.dot_general(left, right, (((1,), (0,)), ((), ())), preferred_element_type=jnp.float32)


def load_pairs(pair_ref):
    chunks = pair_ref.shape[0]
    key_t = jnp.concatenate([pair_ref[j, :HEAD_SIZE, :] for j in range(chunks)], axis=1)
    value_t = jnp.concatenate([pair_ref[j, HEAD_SIZE:, :] for j in range(chunks)], axis=1)
    return key_t, value_t


def flip(block):
    return block.astype(jnp.float32).T.astype(jnp.bfloat16)


def causal_bias(me, keys, width):
    key_pos = lax.broadcasted_iota(jnp.int32, (keys, width), 0)
    query_pos = lax.broadcasted_iota(jnp.int32, (keys, width), 1) + me * width
    return jnp.where(key_pos <= query_pos, 0.0, MASKED)


def attend_kernel(me_ref, query_ref, pair_ref, out_ref, log_ref):
    width = query_ref.shape[1]
    heads = query_ref.shape[0] // HEAD_SIZE
    key_t, value_t = load_pairs(pair_ref)
    key = flip(key_t)
    bias = causal_bias(me_ref[0], key.shape[0], width)
    for h in range(heads):
        rows = slice(h * HEAD_SIZE, (h + 1) * HEAD_SIZE)
        scores = nn_dot(key, query_ref[rows, :]) + bias
        peak = jnp.max(scores, axis=0, keepdims=True)
        soft = jnp.exp(scores - peak)
        total = jnp.sum(soft, axis=0, keepdims=True)
        soft = (soft * (1.0 / total)).astype(jnp.bfloat16)
        out_ref[rows, :] = nn_dot(value_t, soft).astype(jnp.bfloat16)
        log_ref[h : h + 1, :] = peak + jnp.log(total)
    log_ref[heads:, :] = jnp.zeros_like(log_ref[heads:, :])


def attend_back_kernel(me_ref, query_ref, pair_ref, log_ref, grad_ref, query_grad_ref, pair_grad_ref):
    width = query_ref.shape[1]
    heads = query_ref.shape[0] // HEAD_SIZE
    key_t, value_t = load_pairs(pair_ref)
    key, value = flip(key_t), flip(value_t)
    bias = causal_bias(me_ref[0], key.shape[0], width)
    key_grad = jnp.zeros(key.shape, jnp.float32)
    value_grad = jnp.zeros(key.shape, jnp.float32)
    for h in range(heads):
        rows = slice(h * HEAD_SIZE, (h + 1) * HEAD_SIZE)
        query_t, grad_t = query_ref[rows, :], grad_ref[rows, :]
        soft = jnp.exp(nn_dot(key, query_t) + bias - log_ref[h : h + 1, :])
        prob_grad = nn_dot(value, grad_t)
        delta = jnp.sum(soft * prob_grad, axis=0, keepdims=True)
        score_grad = (soft * (prob_grad - delta)).astype(jnp.bfloat16)
        query_grad_ref[rows, :] = nn_dot(key_t, score_grad)
        key_grad = key_grad + nt_dot(score_grad, query_t)
        value_grad = value_grad + nt_dot(soft.astype(jnp.bfloat16), grad_t)
    both = jnp.concatenate([key_grad, value_grad], axis=1).astype(jnp.bfloat16)
    for j in range(pair_grad_ref.shape[0]):
        pair_grad_ref[j] = both[j * width : (j + 1) * width]


def even_attention(query_t, pairs_t, width):
    depth, rows = query_t.shape
    ctx = pairs_t.shape[0]
    me = lax.axis_index("ctx").astype(jnp.int32).reshape(1)
    scalar = pl.BlockSpec(memory_space=pltpu.SMEM)
    wide = pl.BlockSpec((depth, width), lambda s: (0, s))
    pair = pl.BlockSpec((ctx, 2 * HEAD_SIZE, width), lambda s: (0, 0, s))
    logs = pl.BlockSpec((8, width), lambda s: (0, s))
    params = pltpu.CompilerParams(vmem_limit_bytes=VMEM_LIMIT)
    mixed_t, log_total = pl.pallas_call(
        attend_kernel,
        grid=(rows // width,),
        in_specs=[scalar, wide, pair],
        out_specs=[wide, logs],
        out_shape=[
            jax.ShapeDtypeStruct((depth, rows), jnp.bfloat16),
            jax.ShapeDtypeStruct((8, rows), jnp.float32),
        ],
        compiler_params=params,
        name="attend",
    )(me, query_t, pairs_t)

    def back(mixed_back_t):
        return pl.pallas_call(
            attend_back_kernel,
            grid=(rows // width,),
            in_specs=[scalar, wide, pair, logs, wide],
            out_specs=[wide, pl.BlockSpec((ctx, width, 2 * HEAD_SIZE), lambda s: (0, s, 0))],
            out_shape=[
                jax.ShapeDtypeStruct((depth, rows), jnp.float32),
                jax.ShapeDtypeStruct((ctx, rows, 2 * HEAD_SIZE), jnp.bfloat16),
            ],
            compiler_params=params,
            name="attend_back",
        )(me, query_t, pairs_t, log_total, mixed_back_t)

    return mixed_t, back


def ragged_attention(query_t, pairs_t, query_seq, query_pos, pieces):
    ctx = pairs_t.shape[0]
    depth, count_of_rows = query_t.shape
    heads = depth // HEAD_SIZE
    query_rows = query_t.reshape(heads, HEAD_SIZE, count_of_rows).transpose(2, 0, 1)
    pairs = pairs_t.transpose(0, 2, 1).reshape(ctx * count_of_rows, 2 * HEAD_SIZE)
    group_rows = pairs.shape[0]
    key_ids = jnp.arange(group_rows, dtype=jnp.int32)
    key_seq, key_pos = places(key_ids % count_of_rows, key_ids // count_of_rows, pieces)
    key_width = min(512, group_rows)
    block_count = group_rows // key_width

    def scores_at(block_no):
        row_start = block_no * key_width
        pair_rows = lax.dynamic_slice_in_dim(pairs, row_start, key_width, 0)
        seq_part = lax.dynamic_slice_in_dim(key_seq, row_start, key_width, 0)
        pos_part = lax.dynamic_slice_in_dim(key_pos, row_start, key_width, 0)
        allowed = (query_seq[:, None] == seq_part[None, :]) & (
            pos_part[None, :] <= query_pos[:, None]
        )
        key_part = pair_rows[:, :HEAD_SIZE]
        scores = jnp.einsum(
            "qhd,kd->hqk", query_rows, key_part, preferred_element_type=jnp.float32
        )
        return (scores, allowed[None], key_part, pair_rows[:, HEAD_SIZE:])

    def peak_step(block_no, running):
        run_peak, run_total = running
        scores, allowed, key_part, value_part = scores_at(block_no)
        scores = jnp.where(allowed, scores, MASKED)
        new_peak = jnp.maximum(run_peak, jnp.max(scores, axis=-1))
        run_total = run_total * jnp.exp(run_peak - new_peak) + jnp.sum(
            jnp.where(allowed, jnp.exp(scores - new_peak[..., None]), 0.0), axis=-1
        )
        return (new_peak, run_total)

    start_peak = jnp.full((heads, count_of_rows), MASKED, jnp.float32)
    run_peak, run_total = lax.fori_loop(
        0, block_count, peak_step, (start_peak, jnp.zeros_like(start_peak))
    )
    log_total = run_peak + jnp.log(run_total)

    def soft_at(scores, allowed):
        return jnp.where(allowed, jnp.exp(scores - log_total[..., None]), 0.0)

    def output_step(block_no, running):
        scores, allowed, key_part, value_part = scores_at(block_no)
        soft_low = soft_at(scores, allowed).astype(jnp.bfloat16)
        return running + jnp.einsum(
            "hqk,kd->qhd", soft_low, value_part, preferred_element_type=jnp.float32
        )

    attended = lax.fori_loop(
        0, block_count, output_step, jnp.zeros((count_of_rows, heads, HEAD_SIZE), jnp.float32)
    )
    mixed_t = attended.transpose(1, 2, 0).reshape(depth, count_of_rows).astype(jnp.bfloat16)

    def back(mixed_back_t):
        mixed_back = mixed_back_t.reshape(heads, HEAD_SIZE, count_of_rows).transpose(2, 0, 1)
        correction = jnp.einsum("qhd,qhd->hq", mixed_back.astype(jnp.float32), attended)

        def grad_step(block_no, running):
            query_grad, pair_grads = running
            scores, allowed, key_part, value_part = scores_at(block_no)
            soft_part = soft_at(scores, allowed)
            prob_grad = jnp.einsum(
                "qhd,kd->hqk", mixed_back, value_part, preferred_element_type=jnp.float32
            )
            score_grad = (soft_part * (prob_grad - correction[..., None])).astype(jnp.bfloat16)
            query_grad = query_grad + jnp.einsum(
                "hqk,kd->qhd", score_grad, key_part, preferred_element_type=jnp.float32
            )
            key_grad = jnp.einsum(
                "hqk,qhd->kd", score_grad, query_rows, preferred_element_type=jnp.float32
            )
            value_grad = jnp.einsum(
                "hqk,qhd->kd",
                soft_part.astype(jnp.bfloat16),
                mixed_back,
                preferred_element_type=jnp.float32,
            )
            pair_grads = lax.dynamic_update_slice_in_dim(
                pair_grads,
                jnp.concatenate([key_grad, value_grad], axis=-1),
                block_no * key_width,
                0,
            )
            return (query_grad, pair_grads)

        start_grads = (
            jnp.zeros((count_of_rows, heads, HEAD_SIZE), jnp.float32),
            jnp.zeros((group_rows, 2 * HEAD_SIZE), jnp.float32),
        )
        query_grad, pair_grads = lax.fori_loop(0, block_count, grad_step, start_grads)
        query_grad_t = query_grad.transpose(1, 2, 0).reshape(depth, count_of_rows)
        return query_grad_t, pair_grads.astype(jnp.bfloat16).reshape(
            ctx, count_of_rows, 2 * HEAD_SIZE
        )

    return mixed_t, back


def dot32(spec, left, right):
    return jnp.einsum(spec, left, right, preferred_element_type=jnp.float32)


def swap(block):
    return lax.ppermute(block, "tp", [(0, 1), (1, 0)])


def shift(block, axis, k):
    return lax.ppermute(block, axis, [(i, i ^ k) for i in range(lax.axis_size(axis))])


def partner(axis, k):
    return lax.axis_index(axis) ^ k


def pair_sum(partial):
    low = partial.astype(jnp.bfloat16)
    return low.astype(jnp.float32) + swap(low).astype(jnp.float32)


def pair_join(half):
    other = swap(half)
    first = lax.axis_index("tp") == 0
    return jnp.concatenate([jnp.where(first, half, other), jnp.where(first, other, half)], axis=0)


def own_first(rows):
    count = rows.shape[0] // 2
    me = lax.axis_index("tp")
    return (
        lax.dynamic_slice_in_dim(rows, me * count, count, 0),
        lax.dynamic_slice_in_dim(rows, (1 - me) * count, count, 0),
    )


def gather_blocks(block, axis):
    stacked = jnp.zeros((lax.axis_size(axis),) + block.shape, block.dtype)
    for k in range(lax.axis_size(axis)):
        piece = shift(block, axis, k) if k else block
        stacked = lax.dynamic_update_index_in_dim(stacked, piece, partner(axis, k), 0)
    return stacked


def trade_blocks(blocks, axis):
    stacked = jnp.zeros_like(blocks)
    for k in range(lax.axis_size(axis)):
        piece = lax.dynamic_index_in_dim(blocks, partner(axis, k), 0, keepdims=False)
        piece = shift(piece, axis, k) if k else piece
        stacked = lax.dynamic_update_index_in_dim(stacked, piece, partner(axis, k), 0)
    return stacked


def scatter_sum(blocks, axis):
    total = None
    for k in reversed(range(lax.axis_size(axis))):
        piece = lax.dynamic_index_in_dim(blocks, partner(axis, k), 0, keepdims=False)
        piece = (shift(piece, axis, k) if k else piece).astype(jnp.float32)
        total = piece if total is None else total + piece
    return total


def few_partners():
    return lax.axis_size("fsdp") <= 4


def plane_blocks(rows):
    mine, other = own_first(rows)
    if not few_partners():
        return [lax.all_gather(mine, ("fsdp", "tp"), axis=0, tiled=True)]
    blocks = [jnp.concatenate([mine, other], axis=0)]
    for k in range(1, lax.axis_size("fsdp")):
        half = shift(mine, "fsdp", k)
        blocks.append(jnp.concatenate([half, swap(half)], axis=0))
    return blocks


def plane_send(partial, k):
    half = partial.shape[0] // 2
    low = partial.astype(jnp.bfloat16)
    total = partial[:half] + swap(low[half:]).astype(jnp.float32)
    if k:
        total = shift(total.astype(jnp.bfloat16), "fsdp", k).astype(jnp.float32)
    return total


def plane_sum(partials):
    if not few_partners():
        whole = partials(0).astype(jnp.bfloat16)
        return lax.psum_scatter(whole, ("fsdp", "tp"), scatter_dimension=0, tiled=True)
    order = reversed(range(lax.axis_size("fsdp")))
    return sum(plane_send(partials(k), k) for k in order).astype(jnp.bfloat16)


def body(
    tokens,
    cotangent,
    seq_lengths,
    attn_gain,
    qkv_weight,
    joined_bias,
    out_weight,
    mlp_gain,
    gate_up_weight,
    down_weight,
):
    fsdp_size = lax.axis_size("fsdp")
    ctx_size = lax.axis_size("ctx")
    rows = tokens.shape[0]
    part, columns = qkv_weight.shape
    model = part * fsdp_size
    slots = columns // HEAD_SIZE
    heads = slots - 2
    depth = heads * HEAD_SIZE
    bias_part = joined_bias.shape[1]
    hidden_units = down_weight.shape[0]
    lanes = 128 if few_partners() else 8
    ff = -(-hidden_units // (fsdp_size * lanes)) * lanes
    spare = ff * fsdp_size - hidden_units

    small = jnp.concatenate(
        [
            jnp.pad(attn_gain[None], ((0, 0), (0, columns - part))),
            jnp.pad(mlp_gain[None], ((0, 0), (0, columns - part))),
            jnp.pad(joined_bias, ((0, 0), (0, columns - bias_part))),
            jnp.zeros((13, columns), jnp.bfloat16),
        ],
        axis=0,
    )
    packed = gather_blocks(jnp.concatenate([qkv_weight, small], axis=0), "fsdp")
    wide_qkv = packed[:, :part].reshape(model, columns)
    gain_one = packed[:, part, :part].reshape(model).astype(jnp.float32)
    gain_two = packed[:, part + 1, :part].reshape(model).astype(jnp.float32)
    bias_row = packed[:, part + 2, :bias_part].reshape(columns).astype(jnp.float32)

    def sliced(matrix):
        padded = jnp.pad(matrix, ((0, 0), (0, spare)))
        return padded.reshape(part, fsdp_size, ff).transpose(1, 0, 2)

    mlp_parts = jnp.concatenate(
        [sliced(gate_up_weight[:, 0]), sliced(gate_up_weight[:, 1]), sliced(down_weight.T)], axis=2
    )
    mlp_parts, out_part, cot_rows, packed_tie = lax.optimization_barrier(
        (mlp_parts, out_weight.T, cotangent, bias_row)
    )
    bias_row = packed_tie
    wide_out = gather_blocks(out_part, "fsdp").reshape(model, depth)
    wide_mlp = trade_blocks(mlp_parts, "fsdp").reshape(model, 3 * ff)
    wide_gate_up, wide_down = wide_mlp[:, : 2 * ff], wide_mlp[:, 2 * ff :]

    pieces = seq_lengths[0] // ctx_size
    local_rows = jnp.arange(rows, dtype=jnp.int32)
    query_seq, query_pos = places(local_rows, lax.axis_index("ctx"), pieces)
    half = HEAD_SIZE // 2
    frequency = jnp.exp(
        jnp.arange(half, dtype=jnp.float32) * (-2.0 * math.log(THETA) / HEAD_SIZE)
    )
    angles = frequency[:, None] * query_pos.astype(jnp.float32)[None, :]
    cosine, sine = jnp.cos(angles)[None], jnp.sin(angles)[None]

    inputs = tokens.astype(jnp.float32)
    unit_one, inv_one, scaled_one = norm_forward(inputs, gain_one)
    normed_one = scaled_one.astype(jnp.bfloat16)
    projected = dot32("dc,td->ct", wide_qkv, normed_one) + bias_row[:, None]
    projected = projected.reshape(slots, HEAD_SIZE, rows)
    first, second = projected[: heads + 1, :half], projected[: heads + 1, half:]
    turned = jnp.concatenate(
        [first * cosine - second * sine, second * cosine + first * sine], axis=1
    ).astype(jnp.bfloat16)
    query_t = (turned[:heads] * SCORE_SCALE).reshape(depth, rows)
    pair_t = jnp.concatenate([turned[heads], projected[heads + 1].astype(jnp.bfloat16)], axis=0)
    pairs_t = gather_blocks(pair_t, "ctx")
    cot_blocks = plane_blocks(cot_rows)

    seqs = seq_lengths.shape[1]
    if rows * ctx_size == seqs * MIN_SEQ and (rows // seqs) % 128 == 0:
        mixed_t, attention_back = even_attention(query_t, pairs_t, rows // seqs)
    else:
        mixed_t, attention_back = ragged_attention(query_t, pairs_t, query_seq, query_pos, pieces)

    hidden = inputs + pair_sum(dot32("et,de->td", mixed_t, wide_out))
    unit_two, inv_two, scaled_two = norm_forward(hidden, gain_two)
    normed_blocks = plane_blocks(scaled_two.astype(jnp.bfloat16))

    kept = []
    for normed, cot in zip(normed_blocks, cot_blocks):
        gate_up = dot32("td,df->tf", normed, wide_gate_up)
        gate_in, up_in = gate_up[:, :ff], gate_up[:, ff:]
        sigmoid_gate = jax.nn.sigmoid(gate_in)
        act_grad = dot32("td,df->tf", cot, wide_down)
        gate_grad = act_grad * up_in * sigmoid_gate * (1.0 + gate_in * (1.0 - sigmoid_gate))
        up_grad = act_grad * gate_in * sigmoid_gate
        kept.append(
            (
                (gate_in * sigmoid_gate * up_in).astype(jnp.bfloat16),
                jnp.concatenate([gate_grad, up_grad], axis=1).astype(jnp.bfloat16),
            )
        )
    normed_two_grad = plane_sum(lambda k: dot32("tf,df->td", kept[k][1], wide_gate_up))
    normed_all = jnp.concatenate(normed_blocks, axis=0)
    cot_all = jnp.concatenate(cot_blocks, axis=0)
    act_all = jnp.concatenate([item[0] for item in kept], axis=0)
    back_all = jnp.concatenate([item[1] for item in kept], axis=0)

    down_grad = dot32("td,tf->df", cot_all, act_all).astype(jnp.bfloat16)
    gate_up_grad = dot32("td,tf->df", normed_all, back_all).astype(jnp.bfloat16)

    def sum_ctx(grad):
        return lax.psum_scatter(
            grad.reshape(fsdp_size, part, grad.shape[1]), "ctx", scatter_dimension=1, tiled=True
        )

    mlp_grad = jnp.concatenate([sum_ctx(gate_up_grad), sum_ctx(down_grad)], axis=2)
    mlp_grad = trade_blocks(mlp_grad, "fsdp")
    mlp_grad = lax.all_gather(mlp_grad, "ctx", axis=1, tiled=True)

    def joined(lane):
        piece = mlp_grad[:, :, lane * ff : (lane + 1) * ff].transpose(1, 0, 2)
        return piece.reshape(part, fsdp_size * ff)[:, :hidden_units].astype(jnp.float32)

    gate_up_total = jnp.stack([joined(0), joined(1)], axis=1)
    down_total = joined(2).T

    hidden_norm_grad, mlp_gain_grad = norm_backward(
        pair_join(normed_two_grad).astype(jnp.float32),
        unit_two,
        inv_two,
        gain_two,
    )
    hidden_grad = cotangent.astype(jnp.float32) + hidden_norm_grad
    attn_back = hidden_grad.astype(jnp.bfloat16)
    mixed_back_t = dot32("de,td->et", wide_out, attn_back).astype(jnp.bfloat16)
    mixed_back_t, act_list = lax.optimization_barrier((mixed_back_t, [item[0] for item in kept]))
    mlp_out = plane_sum(lambda k: dot32("tf,df->td", act_list[k], wide_down))
    layer_out = (hidden + pair_join(mlp_out).astype(jnp.float32)).astype(jnp.bfloat16)
    out_weight_grad = dot32("td,et->de", attn_back, mixed_t).astype(jnp.bfloat16)
    out_own = scatter_sum(out_weight_grad.reshape(fsdp_size, part, depth), "fsdp")

    query_grad_t, pair_grads = attention_back(mixed_back_t)
    pair_own = scatter_sum(pair_grads, "ctx").T
    turned_grad = jnp.concatenate(
        [query_grad_t.reshape(heads, HEAD_SIZE, rows) * SCORE_SCALE, pair_own[None, :HEAD_SIZE]],
        axis=0,
    )
    first, second = turned_grad[:, :half], turned_grad[:, half:]
    turned_grad = jnp.concatenate(
        [first * cosine + second * sine, second * cosine - first * sine], axis=1
    )
    projected_back = (
        jnp.concatenate([turned_grad, pair_own[None, HEAD_SIZE:]], axis=0)
        .reshape(columns, rows)
        .astype(jnp.bfloat16)
    )
    normed_one_grad = pair_sum(dot32("ct,dc->td", projected_back, wide_qkv))
    input_norm_grad, attn_gain_grad = norm_backward(normed_one_grad, unit_one, inv_one, gain_one)
    token_grad = (hidden_grad + input_norm_grad).astype(jnp.bfloat16)

    qkv_bias_grad = jnp.sum(projected_back, axis=1, dtype=jnp.float32)
    qkv_weight_grad = dot32("td,ct->dc", normed_one, projected_back).astype(jnp.bfloat16)

    def as_rows(vector):
        block = vector.astype(jnp.bfloat16).reshape(fsdp_size, 1, -1)
        return jnp.pad(block, ((0, 0), (0, 0), (0, columns - block.shape[2])))

    tail = jnp.concatenate(
        [
            qkv_weight_grad.reshape(fsdp_size, part, columns),
            as_rows(attn_gain_grad),
            as_rows(mlp_gain_grad),
            as_rows(qkv_bias_grad),
            jnp.zeros((fsdp_size, 13, columns), jnp.bfloat16),
        ],
        axis=1,
    )
    tail_own = jnp.concatenate([scatter_sum(tail, "fsdp")[:part + 16, :], jnp.pad(out_own, ((0, 16), (0, 0)))], axis=1)
    quarter = tail_own.reshape(ctx_size, (part + 16) // ctx_size, columns + depth).astype(jnp.bfloat16)
    quarter = scatter_sum(quarter, "ctx").astype(jnp.bfloat16)
    tail_total = gather_blocks(quarter, "ctx").reshape(part + 16, columns + depth)
    tail_total = tail_total.astype(jnp.float32)
    return (
        layer_out,
        token_grad,
        tail_total[part, :part],
        tail_total[:part, :columns],
        tail_total[part + 2 : part + 3, :bias_part],
        tail_total[:part, columns:].T,
        tail_total[part + 1, :part],
        gate_up_total,
        down_total,
    )


def solution(mesh):
    placed = (
        P(("fsdp", "ctx"), None),
        P(("fsdp", "ctx"), None),
        P("fsdp", None),
        P("fsdp"),
        P("fsdp", "tp"),
        P("tp", "fsdp"),
        P("tp", "fsdp"),
        P("fsdp"),
        P("fsdp", None, "tp"),
        P("tp", "fsdp"),
    )
    return jax.shard_map(
        body,
        mesh=mesh,
        in_specs=placed,
        out_specs=(
            P(("fsdp", "ctx"), None),
            P(("fsdp", "ctx"), None),
            P("fsdp"),
            P("fsdp", "tp"),
            P("tp", "fsdp"),
            P("tp", "fsdp"),
            P("fsdp"),
            P("fsdp", None, "tp"),
            P("tp", "fsdp"),
        ),
        check_vma=False,
    )
```
